32 devices in a mesh: ctx: 16 (over z, y, core), ch: 2 (over x).
Axes of the slice: x: 2, y: 2, z: 4, core: 2. Of those that a mesh axis runs over, the one named last changes fastest.
Arguments:
- tokens: int32 [2048], P('ctx'), may hold values from 0 to 511
- feature_table: bfloat16 [512, 3, 4096], P('ch'), may hold values from -4 to 4
- mr_filter: float32 [128, 256], P(None, 'ch'), may hold values from -4 to 4
- hyena_cot: bfloat16 [2048, 4096], P('ctx', 'ch'), may hold values from -6 to 6
- queries: bfloat16 [2048, 4096], P('ctx', 'ch'), may hold values from -4.5 to 4.5
- keys: bfloat16 [2048, 4096], P('ctx', 'ch'), may hold values from -4.5 to 4.5
- values: bfloat16 [2048, 4096], P('ctx', 'ch'), may hold values from -6 to 6
- attn_cot: bfloat16 [2048, 4096], P('ctx', 'ch'), may hold values from -6 to 6
Outputs:
- hyena_out: bfloat16 [2048, 4096], P('ctx', 'ch')
- feat_grads: bfloat16 [2048, 3, 4096], P('ctx', None, 'ch')
- filter_grad: float32 [128, 256], P(None, 'ch')
- attn_out: bfloat16 [2048, 4096], P('ctx', 'ch')
- queries_grad: bfloat16 [2048, 4096], P('ctx', 'ch')
- keys_grad: bfloat16 [2048, 4096], P('ctx', 'ch')
- values_grad: bfloat16 [2048, 4096], P('ctx', 'ch')
The draws below stay inside these ranges and needn't reach their ends.
All inputs are finite; a program needn't handle non-finite values.
Results may differ from the reference program's by a relative error of at most 0.018.
Values may be sent and summed in bfloat16 or wider, within the bound.
A program may use at most 128 MiB of HBM per device.

```python
import math
import jax
import jax.numpy as jnp
import numpy as np
from jax import lax

VOCAB = 512
CHANNELS = 4096
GROUPS = 256
TAPS = 128
HEADS = 32
HEAD_DIM = 128
TOK_DEV = 128
TOKENS = 2048


def draw_queries(key, part):
    key = jax.random.fold_in(key, 1)
    return jax.random.truncated_normal(key, -4.5, 4.5, (TOKENS, HEADS * HEAD_DIM), jnp.float32).astype(jnp.bfloat16)


def draw_keys(key, part):
    key = jax.random.fold_in(key, 2)
    return jax.random.truncated_normal(key, -4.5, 4.5, (TOKENS, HEADS * HEAD_DIM), jnp.float32).astype(jnp.bfloat16)


def draw_mr_filter(key, part):
    key = jax.random.fold_in(key, 3)
    first, second = jax.random.split(key)
    span = jnp.exp(jax.random.uniform(first, (1, GROUPS), jnp.float32, jnp.log(0.25 * TAPS), jnp.log(8.0 * TAPS)))
    rough = jax.random.truncated_normal(second, -4.0, 4.0, (TAPS, GROUPS), jnp.float32)
    ratio = jnp.exp(-1.0 / span)
    lags = jnp.arange(TAPS, dtype=jnp.float32)[:, None]
    amplitude = jnp.sqrt((1.0 - ratio ** 2) / (1.0 - ratio ** (2 * TAPS)))
    return rough * amplitude * ratio ** lags


def place_ends(entries, key, least, high):
    spot = [jax.random.randint(jax.random.fold_in(key, axis), (), 0, length) for axis, length in enumerate(entries.shape)]
    main_axis = entries.shape.index(max(entries.shape))
    neighbour = spot[:main_axis] + [(spot[main_axis] + 1) % entries.shape[main_axis]] + spot[main_axis + 1:]
    return entries.at[tuple(spot)].set(least).at[tuple(neighbour)].set(high)


def level_of(own_key, extent, cuts, smallest, top_value):
    def one(dim, blocks):
        heights = jax.random.uniform(jax.random.fold_in(jax.random.fold_in(own_key, 6), dim), (blocks,), jnp.float32, smallest / len(cuts), top_value / len(cuts))
        return jnp.repeat(jnp.exp(heights), extent[dim] // blocks).reshape((-1,) + (1,) * (len(extent) - dim - 1))

    factor_of = one(*cuts[0])
    for cut in cuts[1:]:
        factor_of = factor_of * one(*cut)
    return factor_of


def rank_bounds(number_of, lean):
    loads = [(1 << 20) // math.isqrt(standing ** lean) + 1 for standing in range(1, number_of + 1)]
    deviation = 1 + sum(loads) // (1 << 30)
    return np.cumsum(np.array([max(1, weight // deviation) for weight in loads]))


def skewed_ids(stream_key, dims, amount, skew):
    listing = rank_bounds(amount, skew)
    pick = jax.random.randint(jax.random.fold_in(stream_key, 1), dims, 0, int(listing[amount - 1]))
    grade = jnp.searchsorted(jnp.asarray(listing, jnp.int32), pick, side="right")
    return jax.random.permutation(jax.random.fold_in(stream_key, 2), amount)[grade].astype(jnp.int32)


def bell_draw(rng, dims, scale, most, pieces=(), kind=jnp.bfloat16):
    values = scale * jax.random.normal(rng, dims, jnp.float32)
    if pieces:
        values = values * level_of(rng, dims, pieces, -0.22, 0.18)
    return jnp.clip(values, -most, most).astype(kind)


def setup_inputs(seed: int = 0) -> dict:
    splits = jax.random.split(jax.random.key(seed), 9)
    tokens = place_ends(skewed_ids(splits[0], (TOKENS,), VOCAB, 2), jax.random.fold_in(splits[0], 3), 0, VOCAB - 1).astype(jnp.int32)
    feature_table = bell_draw(splits[1], (VOCAB, 3, CHANNELS), 1.0, 4.0, ((0, 2),))
    mr_filter = draw_mr_filter(jax.random.fold_in(splits[8], 71), 0)
    hyena_cot = bell_draw(splits[3], (TOKENS, CHANNELS), 1.0, 6.0, ((0, 16), (1, 2)))
    queries = draw_queries(jax.random.fold_in(splits[8], 71), 0)
    keys = draw_keys(jax.random.fold_in(splits[8], 71), 0)
    values = bell_draw(splits[6], (TOKENS, HEADS * HEAD_DIM), 1.0, 6.0, ((0, 16), (1, 2)))
    attn_cot = bell_draw(splits[7], (TOKENS, HEADS * HEAD_DIM), 1.0, 6.0, ((0, 16), (1, 2)))
    return {"tokens": tokens, "feature_table": feature_table, "mr_filter": mr_filter, "hyena_cot": hyena_cot, "queries": queries, "keys": keys, "values": values, "attn_cot": attn_cot}


NEG = -1e+30

def causal_conv(signal, filt):
    block = TOK_DEV
    count = TOKENS // block
    per_group = CHANNELS // GROUPS
    padded = jnp.pad(signal, ((block, 0), (0, 0)))
    current = padded[block:].reshape(count, block, GROUPS, per_group)
    previous = padded[:TOKENS].reshape(count, block, GROUPS, per_group)
    window = jnp.concatenate([previous, current], 1)
    row_ids = jnp.arange(block, dtype=jnp.int32)[:, None]
    col_ids = jnp.arange(2 * block, dtype=jnp.int32)[None, :]
    lag = row_ids - col_ids + block
    valid = (lag >= 0) & (lag < TAPS)
    taken = filt[jnp.clip(lag, 0, TAPS - 1)]
    kernel = jnp.where(valid[:, :, None], taken, jnp.zeros_like(taken))
    result = jnp.einsum('ikg,nkgc->nigc', kernel, window, precision=lax.Precision.HIGHEST)
    return result.reshape(TOKENS, CHANNELS)

def hyena_part(tokens, feature_table, mr_filter, hyena_cot):
    features = feature_table[tokens]
    gate_in = features[:, 0].astype(jnp.float32)
    gate_out = features[:, 1].astype(jnp.float32)
    value_in = features[:, 2].astype(jnp.float32)
    mixed = (gate_in * value_in).astype(jnp.bfloat16)
    long_conv, pullback = jax.vjp(causal_conv, mixed.astype(jnp.float32), mr_filter.astype(jnp.float32))
    hyena_out = (gate_out * long_conv).astype(jnp.bfloat16)
    cotangent = hyena_cot.astype(jnp.float32)
    conv_cot = (cotangent * gate_out).astype(jnp.bfloat16)
    mixed_grad, filter_grad = pullback(conv_cot.astype(jnp.float32))
    feat_grads = jnp.stack([(mixed_grad * value_in).astype(jnp.bfloat16), (cotangent * long_conv).astype(jnp.bfloat16), (mixed_grad * gate_in).astype(jnp.bfloat16)], axis=1)
    return (hyena_out, feat_grads, filter_grad)

def attend_head(operands):
    query_rows, key_rows, value_rows, cot_rows = operands
    length = query_rows.shape[0]
    block = math.gcd(length, 1024)
    scale = HEAD_DIM ** (-0.5)
    outputs = []
    query_grads = []
    key_grad = jnp.zeros((length, HEAD_DIM), jnp.float32)
    value_grad = jnp.zeros((length, HEAD_DIM), jnp.float32)
    for number in range(length // block):
        start = number * block
        finish = start + block
        query_block = query_rows[start:finish]
        cot_block = cot_rows[start:finish]
        key_part = key_rows[:finish]
        value_part = value_rows[:finish]
        query_pos = start + jnp.arange(block, dtype=jnp.int32)
        key_pos = jnp.arange(finish, dtype=jnp.int32)
        allowed = key_pos[None, :] <= query_pos[:, None]
        scores = jnp.dot(query_block, key_part.T, preferred_element_type=jnp.float32) * scale
        scores = jnp.where(allowed, scores, NEG)
        row_max = scores.max(axis=1)
        probs_raw = jnp.where(allowed, jnp.exp(scores - row_max[:, None]), 0.0)
        row_total = probs_raw.sum(axis=1)
        weighted = jnp.dot(probs_raw.astype(jnp.bfloat16), value_part, preferred_element_type=jnp.float32)
        output = (weighted / row_total[:, None]).astype(jnp.bfloat16)
        log_total = row_max + jnp.log(row_total)
        delta = lax.optimization_barrier(jnp.sum(cot_block.astype(jnp.float32) * output.astype(jnp.float32), axis=1))
        probs = jnp.where(allowed, jnp.exp(scores - log_total[:, None]), 0.0)
        value_grad = value_grad.at[:finish].add(jnp.dot(probs.astype(jnp.bfloat16).T, cot_block, preferred_element_type=jnp.float32))
        dprobs = jnp.dot(cot_block, value_part.T, preferred_element_type=jnp.float32)
        dscores = (probs * (dprobs - delta[:, None])).astype(jnp.bfloat16)
        query_grads.append((jnp.dot(dscores, key_part, preferred_element_type=jnp.float32) * scale).astype(jnp.bfloat16))
        key_grad = key_grad.at[:finish].add(jnp.dot(dscores.T, query_block, preferred_element_type=jnp.float32) * scale)
        outputs.append(output)
    return (jnp.concatenate(outputs, 0), jnp.concatenate(query_grads, 0), key_grad.astype(jnp.bfloat16), value_grad.astype(jnp.bfloat16))

def by_heads(array):
    return jnp.transpose(array.reshape(TOKENS, HEADS, HEAD_DIM), (1, 0, 2))

def by_rows(array):
    return jnp.transpose(array, (1, 0, 2)).reshape(TOKENS, HEADS * HEAD_DIM)

def reference(tokens, feature_table, mr_filter, hyena_cot, queries, keys, values, attn_cot):
    hyena_out, feat_grads, filter_grad = hyena_part(tokens, feature_table, mr_filter, hyena_cot)
    results = lax.map(attend_head, (by_heads(queries), by_heads(keys), by_heads(values), by_heads(attn_cot)))
    attn_out, queries_grad, keys_grad, values_grad = [by_rows(item) for item in results]
    return (hyena_out, feat_grads, filter_grad, attn_out, queries_grad, keys_grad, values_grad)
```

```python
import jax
import jax.numpy as jnp
from jax import lax
from jax.experimental import pallas as pl
from jax.experimental.pallas import tpu as pltpu
from jax.sharding import PartitionSpec as P

HEAD_DIM = 128


NEG = -1e30


def from_partner(shard, axis, apart):
    return lax.ppermute(shard, axis, [(i, i ^ 1 << apart) for i in range(lax.axis_size(axis))])


def passed_along(value, axis, steps):
    count = lax.axis_size(axis)
    leading, last = (max(0, -steps), min(count, count - steps))
    return lax.ppermute(value, axis, [(source, source + steps) for source in range(leading, last)])


def from_behind(shard, axis, by):
    peers = lax.axis_size(axis)
    return lax.ppermute(shard, axis, [(i, (i + by) % peers) for i in range(peers)])


def heads_in(stacked, position, bit):
    width = stacked.shape[2] // 2
    upper = position // (1 << bit) % 2 == 1
    lower_heads = stacked[:, :, :width]
    upper_heads = stacked[:, :, width:]
    kept = jnp.where(upper, upper_heads, lower_heads)
    given = jnp.where(upper, lower_heads, upper_heads)
    received = from_partner(given, "ctx", bit)
    return jnp.concatenate([jnp.where(upper, received, kept), jnp.where(upper, kept, received)], 1)


def heads_out(stacked, position, bit):
    length = stacked.shape[1] // 2
    upper = position // (1 << bit) % 2 == 1
    lower_rows = stacked[:, :length]
    upper_rows = stacked[:, length:]
    kept = jnp.where(upper, upper_rows, lower_rows)
    given = jnp.where(upper, lower_rows, upper_rows)
    received = from_partner(given, "ctx", bit)
    return jnp.concatenate([jnp.where(upper, received, kept), jnp.where(upper, kept, received)], 2)


def fold_rows(stacked, bits):
    length = stacked.shape[1] // 2
    moving = stacked[:, length:]
    for bit in range(2, bits):
        moving = from_partner(moving, "ctx", bit)
    return jnp.concatenate([stacked[:, :length], moving], 1)


def block_starts(group, length, group_count):
    return (2 * group * length, (2 * group_count - 1 - 2 * group) * length)


def masked_scores(query_block, key_block, query_start, key_start, scale):
    query_pos = query_start + lax.iota(jnp.int32, query_block.shape[0])
    key_pos = key_start + lax.iota(jnp.int32, key_block.shape[0])
    allowed = (key_pos[None, :] <= query_pos[:, None])[None]
    scores = (
        jnp.einsum("qhd,khd->hqk", query_block, key_block, preferred_element_type=jnp.float32)
        * scale
    )
    return (allowed, jnp.where(allowed, scores, NEG))


def keep_state(state):
    return state


def forward_tile(state, query_block, query_start, key_block, value_block, key_start, scale):

    def forward_work(state):
        running_max, running_total, weighted = state
        allowed, scores = masked_scores(query_block, key_block, query_start, key_start, scale)
        new_max = jnp.maximum(running_max, scores.max(axis=-1))
        weights = jnp.where(allowed, jnp.exp(scores - new_max[..., None]), 0.0)
        shrink = jnp.exp(running_max - new_max)
        running_total = running_total * shrink + weights.sum(axis=-1)
        weighted = weighted * shrink[..., None] + jnp.einsum(
            "hqk,khd->hqd",
            weights.astype(jnp.bfloat16),
            value_block,
            preferred_element_type=jnp.float32,
        )
        return (new_max, running_total, weighted)

    return lax.cond(key_start < query_start + query_block.shape[0], forward_work, keep_state, state)


def query_grad_tile(
    query_grad,
    query_block,
    cot_block,
    log_total,
    delta,
    query_start,
    key_block,
    value_block,
    key_start,
    scale,
):

    def query_work(query_grad):
        allowed, scores = masked_scores(query_block, key_block, query_start, key_start, scale)
        probs = jnp.where(allowed, jnp.exp(scores - log_total[..., None]), 0.0)
        dprobs = jnp.einsum(
            "qhd,khd->hqk", cot_block, value_block, preferred_element_type=jnp.float32
        )
        dscores = (probs * (dprobs - delta[..., None])).astype(jnp.bfloat16)
        return (
            query_grad
            + jnp.einsum("hqk,khd->hqd", dscores, key_block, preferred_element_type=jnp.float32)
            * scale
        )

    return lax.cond(
        key_start < query_start + query_block.shape[0], query_work, keep_state, query_grad
    )


def key_grad_tile(
    grads,
    query_block,
    cot_block,
    log_total,
    delta,
    query_start,
    key_block,
    value_block,
    key_start,
    scale,
):

    def key_work(grads):
        key_grad, value_grad = grads
        allowed, scores = masked_scores(query_block, key_block, query_start, key_start, scale)
        probs = jnp.where(allowed, jnp.exp(scores - log_total[..., None]), 0.0)
        value_grad = value_grad + jnp.einsum(
            "hqk,qhd->hkd",
            probs.astype(jnp.bfloat16),
            cot_block,
            preferred_element_type=jnp.float32,
        )
        dprobs = jnp.einsum(
            "qhd,khd->hqk", cot_block, value_block, preferred_element_type=jnp.float32
        )
        dscores = (probs * (dprobs - delta[..., None])).astype(jnp.bfloat16)
        key_grad = (
            key_grad
            + jnp.einsum("hqk,qhd->hkd", dscores, query_block, preferred_element_type=jnp.float32)
            * scale
        )
        return (key_grad, value_grad)

    return lax.cond(key_start < query_start + query_block.shape[0], key_work, keep_state, grads)


LANES = 128


def dot(left, right, left_dim, right_dim):
    return lax.dot_general(
        left, right, (((left_dim,), (right_dim,)), ((), ())), preferred_element_type=jnp.float32
    )


def hyena_kernel(
    per_group, mixed, earlier, conv_cot, later, gate_in, gate_out, value_in, cot,
    back_rows, ahead_rows, hyena_out, grad_in, grad_out, grad_value, filter_part,
):
    rows = mixed.shape[0]
    span = 2 * rows
    window = jnp.concatenate([earlier[...], mixed[...]], 0)
    cot_here = conv_cot[...]
    ahead = jnp.concatenate([cot_here, later[...]], 0)
    row_id = lax.broadcasted_iota(jnp.int32, (rows, rows), 0)
    col_id = lax.broadcasted_iota(jnp.int32, (rows, rows), 1)
    flip = (row_id + col_id == rows - 1).astype(jnp.float32).astype(jnp.bfloat16)
    flipped = dot(flip, cot_here, 1, 0)
    lane_group = lax.broadcasted_iota(jnp.int32, (rows, LANES), 1) // per_group
    long_conv = jnp.zeros((rows, LANES), jnp.float32)
    mixed_grad = jnp.zeros((rows, LANES), jnp.float32)

    def toeplitz(row):
        spread = jnp.broadcast_to(row, (rows, span))
        return pltpu.roll(spread, 0, 1, stride=1, stride_axis=0).astype(jnp.bfloat16)

    for number in range(LANES // per_group):
        mine = lane_group == number
        back = toeplitz(back_rows[0, number : number + 1, :])
        long_conv = jnp.where(mine, dot(back, window, 1, 0), long_conv)
        forward = toeplitz(ahead_rows[0, number : number + 1, :])
        mixed_grad = jnp.where(mine, dot(forward, ahead, 1, 0), mixed_grad)
        picked = jnp.where(mine, flipped, 0.0).astype(jnp.bfloat16)
        products = dot(picked, window, 1, 1)
        aligned = pltpu.roll(products, 0, 1, stride=1, stride_axis=0)
        filter_part[0, number : number + 1, :] = jnp.sum(aligned, axis=0, keepdims=True)
    hyena_out[...] = (gate_out[...].astype(jnp.float32) * long_conv).astype(jnp.bfloat16)
    grad_in[...] = (mixed_grad * value_in[...].astype(jnp.float32)).astype(jnp.bfloat16)
    grad_out[...] = (cot[...].astype(jnp.float32) * long_conv).astype(jnp.bfloat16)
    grad_value[...] = (mixed_grad * gate_in[...].astype(jnp.float32)).astype(jnp.bfloat16)


def hyena(mixed, earlier, conv_cot, later, gate_in, gate_out, value_in, cot, mr_filter):
    rows, channels = mixed.shape
    taps, groups = mr_filter.shape
    per_group = channels // groups
    per_step = LANES // per_group
    steps = channels // LANES
    span = 2 * rows
    by_group = mr_filter.T
    blank = jnp.zeros((groups, span - taps), jnp.float32)
    back_rows = jnp.concatenate([blank[:, :1], by_group[:, ::-1], blank[:, 1:]], 1)
    ahead_rows = jnp.concatenate([by_group, blank], 1)
    block = pl.BlockSpec((rows, LANES), lambda step: (0, step))
    per = pl.BlockSpec((1, per_step, span), lambda step: (step, 0, 0))

    def body(*refs):
        hyena_kernel(per_group, *refs)

    wide = jax.ShapeDtypeStruct((rows, channels), jnp.bfloat16)
    *outs, parts = pl.pallas_call(
        body,
        grid=(steps,),
        in_specs=[block] * 8 + [per] * 2,
        out_specs=[block] * 4 + [per],
        out_shape=[wide] * 4 + [jax.ShapeDtypeStruct((steps, per_step, span), jnp.float32)],
        cost_estimate=pl.CostEstimate(
            flops=12 * rows * span * channels * per_step, bytes_accessed=12 * rows * channels * 2,
            transcendentals=0,
        ),
        compiler_params=pltpu.CompilerParams(vmem_limit_bytes=32 * 1024 * 1024),
    )(
        mixed, earlier, conv_cot, later, gate_in, gate_out, value_in, cot,
        back_rows.reshape(steps, per_step, span), ahead_rows.reshape(steps, per_step, span),
    )
    local_grad = parts.reshape(groups, span)[:, span - taps :][:, ::-1].T
    return outs, local_grad


def attention_kernel(block, arrays, results, keys_across, values_across, cots_across, key_sum, value_sum):
    count, _, length, _ = arrays.shape
    total = count * length
    scale = HEAD_DIM ** (-0.5)
    per = block // length

    def take(which, first, last):
        return arrays[first:last, which].reshape((last - first) * length, HEAD_DIM)

    def put(which, first, last, value):
        results[first:last, which] = value.astype(jnp.bfloat16).reshape(
            last - first, length, HEAD_DIM
        )

    keys_across[...] = take(1, 0, count).T
    values_across[...] = take(2, 0, count).T
    cots_across[...] = take(3, 0, count).T
    key_row = lax.broadcasted_iota(jnp.int32, (block, block), 0)
    query_col = lax.broadcasted_iota(jnp.int32, (block, block), 1)
    allowed = key_row <= query_col
    for step in reversed(range(total // block)):
        first, last = step * per, (step + 1) * per
        here = slice(step * block, (step + 1) * block)
        queries, cots = take(0, first, last), take(3, first, last)
        pieces = []
        for part in range(step + 1):
            piece = dot(take(1, part * per, (part + 1) * per), queries, 1, 1) * scale
            pieces.append(jnp.where(allowed, piece, NEG) if part == step else piece)
        row_max = pieces[0].max(axis=0, keepdims=True)
        for piece in pieces[1:]:
            row_max = jnp.maximum(row_max, piece.max(axis=0, keepdims=True))
        probs = [jnp.exp(piece - row_max) for piece in pieces]
        row_total = probs[0].sum(axis=0, keepdims=True)
        for piece in probs[1:]:
            row_total = row_total + piece.sum(axis=0, keepdims=True)
        weighted = None
        for part, piece in enumerate(probs):
            span = slice(part * block, (part + 1) * block)
            term = dot(values_across[:, span], piece.astype(jnp.bfloat16), 1, 0)
            weighted = term if weighted is None else weighted + term
        inverse = 1.0 / row_total
        output = (weighted * inverse).astype(jnp.bfloat16).astype(jnp.float32)
        put(0, first, last, output.T)
        delta = jnp.sum(cots_across[:, here].astype(jnp.float32) * output, axis=0, keepdims=True)
        query_grad = None
        for part, piece in enumerate(probs):
            span = slice(part * block, (part + 1) * block)
            piece = piece * inverse
            value_term = dot(piece.astype(jnp.bfloat16), cots, 1, 0)
            dprobs = dot(take(2, part * per, (part + 1) * per), cots, 1, 1)
            dscores = (piece * (dprobs - delta)).astype(jnp.bfloat16)
            key_term = dot(dscores, queries, 1, 0)
            if step == total // block - 1:
                value_sum[span], key_sum[span] = value_term, key_term
            else:
                value_sum[span] += value_term
                key_sum[span] += key_term
            term = dot(keys_across[:, span], dscores, 1, 0)
            query_grad = term if query_grad is None else query_grad + term
        put(1, first, last, (query_grad * scale).T)
    put(2, 0, count, key_sum[...] * scale)
    put(3, 0, count, value_sum[...])


def whole_head(queries, keys, values, attn_cot):
    peers = lax.axis_size("ctx")
    length, width = queries.shape
    split = [
        array.reshape(length, peers, HEAD_DIM).transpose(1, 0, 2)
        for array in (queries, keys, values, attn_cot)
    ]
    arrays = lax.all_to_all(jnp.stack(split, 1), "ctx", 0, 0)
    total = peers * length
    across = pltpu.VMEM((HEAD_DIM, total), jnp.bfloat16)
    down = pltpu.VMEM((total, HEAD_DIM), jnp.float32)

    def body(*refs):
        attention_kernel(2 * length, *refs)

    results = pl.pallas_call(
        body,
        in_specs=[pl.BlockSpec(memory_space=pltpu.VMEM)],
        out_specs=pl.BlockSpec(memory_space=pltpu.VMEM),
        out_shape=jax.ShapeDtypeStruct(arrays.shape, jnp.bfloat16),
        scratch_shapes=[across] * 3 + [down] * 2,
        cost_estimate=pl.CostEstimate(
            flops=7 * total * total * HEAD_DIM, bytes_accessed=16 * total * HEAD_DIM,
            transcendentals=total * total // 2,
        ),
        compiler_params=pltpu.CompilerParams(vmem_limit_bytes=48 * 1024 * 1024),
    )(arrays)
    results = lax.all_to_all(results, "ctx", 0, 0)
    return [results[:, which].transpose(1, 0, 2).reshape(length, width) for which in range(4)]


def ring_attention(queries, keys, values, attn_cot):
    position = lax.axis_index("ctx")
    stacked = jnp.stack([queries, keys, values, attn_cot])
    for bit in (0, 1):
        stacked = heads_in(stacked, position, bit)
    bits = lax.axis_size("ctx").bit_length() - 1
    stacked = fold_rows(stacked, bits)
    rows = stacked.shape[1]
    length = rows // 2
    heads_here = stacked.shape[2] // HEAD_DIM
    split = stacked.reshape(4, rows, heads_here, HEAD_DIM)
    query_here = split[0]
    key_here = split[1]
    value_here = split[2]
    cot_here = split[3]
    group_count = lax.axis_size("ctx") // 4
    group = position // 4
    mine = block_starts(group, length, group_count)
    scale = HEAD_DIM ** (-0.5)
    query_blocks = (query_here[:length], query_here[length:])
    cot_blocks = (cot_here[:length], cot_here[length:])

    def forward_visit(states, pair, source):
        theirs = block_starts(source, length, group_count)
        updated = []
        for query_side in (0, 1):
            state = states[query_side]
            for key_side in (0, 1):
                state = forward_tile(
                    state,
                    query_blocks[query_side],
                    mine[query_side],
                    pair[0, key_side * length : (key_side + 1) * length],
                    pair[1, key_side * length : (key_side + 1) * length],
                    theirs[key_side],
                    scale,
                )
            updated.append(state)
        return tuple(updated)

    empty = (
        jnp.full((heads_here, length), NEG, jnp.float32),
        jnp.zeros((heads_here, length), jnp.float32),
        jnp.zeros((heads_here, length, HEAD_DIM), jnp.float32),
    )
    pair = jnp.stack([key_here, value_here])
    saved = jnp.zeros((group_count,) + pair.shape, jnp.bfloat16)

    def forward_step(step, carry):
        states, saved, pair = carry
        states = forward_visit(states, pair, (group - step) % group_count)
        saved = lax.dynamic_update_index_in_dim(saved, pair, step, 0)
        pair = from_behind(pair, "ctx", 4)
        return (states, saved, pair)

    states, saved, pair = lax.fori_loop(
        0, group_count - 1, forward_step, ((empty, empty), saved, pair)
    )
    final_step = group_count - 1
    states = forward_visit(states, pair, (group - final_step) % group_count)
    saved = lax.dynamic_update_index_in_dim(saved, pair, final_step, 0)
    out_blocks = []
    log_totals = []
    deltas = []
    for query_side in (0, 1):
        running_max, running_total, weighted = states[query_side]
        output = (weighted / running_total[..., None]).astype(jnp.bfloat16)
        out_blocks.append(output)
        log_totals.append(running_max + jnp.log(running_total))
        cot_heads = jnp.transpose(cot_blocks[query_side], (1, 0, 2)).astype(jnp.float32)
        deltas.append(jnp.sum(cot_heads * output.astype(jnp.float32), axis=-1))
    zero_grad = jnp.zeros((heads_here, length, HEAD_DIM), jnp.float32)

    def query_step(step, grads):
        pair = lax.dynamic_index_in_dim(saved, step, 0, keepdims=False)
        theirs = block_starts((group - step) % group_count, length, group_count)
        updated = []
        for query_side in (0, 1):
            current = grads[query_side]
            for key_side in (0, 1):
                current = query_grad_tile(
                    current,
                    query_blocks[query_side],
                    cot_blocks[query_side],
                    log_totals[query_side],
                    deltas[query_side],
                    mine[query_side],
                    pair[0, key_side * length : (key_side + 1) * length],
                    pair[1, key_side * length : (key_side + 1) * length],
                    theirs[key_side],
                    scale,
                )
            updated.append(current)
        return tuple(updated)

    query_grads = lax.fori_loop(0, group_count, query_step, (zero_grad, zero_grad))

    def key_visit(grads, packed, log_all, delta_all, source):
        theirs = block_starts(source, length, group_count)
        updated = []
        for key_side in (0, 1):
            current = grads[key_side]
            for query_side in (0, 1):
                current = key_grad_tile(
                    current,
                    packed[0, query_side * length : (query_side + 1) * length],
                    packed[1, query_side * length : (query_side + 1) * length],
                    log_all[query_side],
                    delta_all[query_side],
                    theirs[query_side],
                    key_here[key_side * length : (key_side + 1) * length],
                    value_here[key_side * length : (key_side + 1) * length],
                    mine[key_side],
                    scale,
                )
            updated.append(current)
        return tuple(updated)

    def key_step(step, carry):
        grads, packed, log_all, delta_all = carry
        grads = key_visit(grads, packed, log_all, delta_all, (group - step) % group_count)
        packed = from_behind(packed, "ctx", 4)
        log_all, delta_all = from_behind((log_all, delta_all), "ctx", 4)
        return (grads, packed, log_all, delta_all)

    start_grads = ((zero_grad, zero_grad), (zero_grad, zero_grad))
    packed = jnp.stack([query_here, cot_here])
    carry = (start_grads, packed, jnp.stack(log_totals), jnp.stack(deltas))
    grads, packed, log_all, delta_all = lax.fori_loop(0, group_count - 1, key_step, carry)
    grads = key_visit(grads, packed, log_all, delta_all, (group - final_step) % group_count)

    def joined_rows(first_block, second_block):
        whole = jnp.concatenate([first_block, second_block], 1)
        return jnp.transpose(whole, (1, 0, 2)).reshape(rows, -1).astype(jnp.bfloat16)

    result = jnp.stack(
        [
            joined_rows(out_blocks[0], out_blocks[1]),
            joined_rows(query_grads[0], query_grads[1]),
            joined_rows(grads[0][0], grads[1][0]),
            joined_rows(grads[0][1], grads[1][1]),
        ]
    )
    result = fold_rows(result, bits)
    for bit in (1, 0):
        result = heads_out(result, position, bit)
    return result[0], result[1], result[2], result[3]


def summed_over(value, axis):
    step = 1
    while step < lax.axis_size(axis):
        pairs = [(i, i ^ step) for i in range(lax.axis_size(axis))]
        value = value + lax.ppermute(value, axis, pairs)
        step *= 2
    return value


def looked_up(tokens, feature_table):
    vocab_part = feature_table.shape[0]
    first_id = lax.axis_index("ch") * vocab_part
    matches = tokens[:, None] == first_id + lax.iota(jnp.int32, vocab_part)[None, :]
    matches = matches.astype(jnp.bfloat16)
    partial = jnp.einsum(
        "tv,vic->itc", matches, feature_table, preferred_element_type=jnp.float32
    ).astype(jnp.bfloat16)
    peers = lax.axis_size("ch")
    if peers != 2:
        return lax.psum_scatter(partial, "ch", scatter_dimension=2, tiled=True)
    width = partial.shape[2] // 2
    upper = lax.axis_index("ch") == 1
    low, high = partial[:, :, :width], partial[:, :, width:]
    given = jnp.where(upper, low, high)
    return jnp.where(upper, high, low) + lax.ppermute(given, "ch", [(0, 1), (1, 0)])


def local(tokens, feature_table, mr_filter, hyena_cot, queries, keys, values, attn_cot):
    gate_in, gate_out, value_in = looked_up(tokens, feature_table)
    mixed = (gate_in.astype(jnp.float32) * value_in.astype(jnp.float32)).astype(jnp.bfloat16)
    conv_cot = (hyena_cot.astype(jnp.float32) * gate_out.astype(jnp.float32)).astype(jnp.bfloat16)
    earlier = passed_along(mixed, "ctx", 1)
    later = passed_along(conv_cot, "ctx", -1)
    outs, local_grad = hyena(
        mixed, earlier, conv_cot, later, gate_in, gate_out, value_in, hyena_cot, mr_filter
    )
    feat_grads = jnp.stack(outs[1:], axis=1)
    filter_grad = summed_over(local_grad, "ctx")
    if queries.shape[1] == lax.axis_size("ctx") * HEAD_DIM:
        attention = whole_head(queries, keys, values, attn_cot)
    else:
        attention = ring_attention(queries, keys, values, attn_cot)
    return (outs[0], feat_grads, filter_grad, *attention)


def solution(mesh):
    return jax.shard_map(
        local,
        mesh=mesh,
        in_specs=(
            P("ctx"),
            P("ch", None, None),
            P(None, "ch"),
            P("ctx", "ch"),
            P("ctx", "ch"),
            P("ctx", "ch"),
            P("ctx", "ch"),
            P("ctx", "ch"),
        ),
        out_specs=(
            P("ctx", "ch"),
            P("ctx", None, "ch"),
            P(None, "ch"),
            P("ctx", "ch"),
            P("ctx", "ch"),
            P("ctx", "ch"),
            P("ctx", "ch"),
        ),
        check_vma=False,
    )
```

```python
import jax
import jax.numpy as jnp
from jax import lax
from jax.experimental import pallas as pl
from jax.experimental.pallas import tpu as pltpu
from jax.sharding import PartitionSpec as P

HEAD_DIM = 128


NEG = -1e30


def from_partner(shard, axis, apart):
    return lax.ppermute(shard, axis, [(i, i ^ 1 << apart) for i in range(lax.axis_size(axis))])


def passed_along(value, axis, steps):
    count = lax.axis_size(axis)
    leading, last = (max(0, -steps), min(count, count - steps))
    return lax.ppermute(value, axis, [(source, source + steps) for source in range(leading, last)])


def from_behind(shard, axis, by):
    peers = lax.axis_size(axis)
    return lax.ppermute(shard, axis, [(i, (i + by) % peers) for i in range(peers)])


def heads_in(stacked, position, bit):
    width = stacked.shape[2] // 2
    upper = position // (1 << bit) % 2 == 1
    lower_heads = stacked[:, :, :width]
    upper_heads = stacked[:, :, width:]
    kept = jnp.where(upper, upper_heads, lower_heads)
    given = jnp.where(upper, lower_heads, upper_heads)
    received = from_partner(given, "ctx", bit)
    return jnp.concatenate([jnp.where(upper, received, kept), jnp.where(upper, kept, received)], 1)


def heads_out(stacked, position, bit):
    length = stacked.shape[1] // 2
    upper = position // (1 << bit) % 2 == 1
    lower_rows = stacked[:, :length]
    upper_rows = stacked[:, length:]
    kept = jnp.where(upper, upper_rows, lower_rows)
    given = jnp.where(upper, lower_rows, upper_rows)
    received = from_partner(given, "ctx", bit)
    return jnp.concatenate([jnp.where(upper, received, kept), jnp.where(upper, kept, received)], 2)


def fold_rows(stacked, bits):
    length = stacked.shape[1] // 2
    moving = stacked[:, length:]
    for bit in range(2, bits):
        moving = from_partner(moving, "ctx", bit)
    return jnp.concatenate([stacked[:, :length], moving], 1)


def block_starts(group, length, group_count):
    return (2 * group * length, (2 * group_count - 1 - 2 * group) * length)


def masked_scores(query_block, key_block, query_start, key_start, scale):
    query_pos = query_start + lax.iota(jnp.int32, query_block.shape[0])
    key_pos = key_start + lax.iota(jnp.int32, key_block.shape[0])
    allowed = (key_pos[None, :] <= query_pos[:, None])[None]
    scores = (
        jnp.einsum("qhd,khd->hqk", query_block, key_block, preferred_element_type=jnp.float32)
        * scale
    )
    return (allowed, jnp.where(allowed, scores, NEG))


def keep_state(state):
    return state


def forward_tile(state, query_block, query_start, key_block, value_block, key_start, scale):

    def forward_work(state):
        running_max, running_total, weighted = state
        allowed, scores = masked_scores(query_block, key_block, query_start, key_start, scale)
        new_max = jnp.maximum(running_max, scores.max(axis=-1))
        weights = jnp.where(allowed, jnp.exp(scores - new_max[..., None]), 0.0)
        shrink = jnp.exp(running_max - new_max)
        running_total = running_total * shrink + weights.sum(axis=-1)
        weighted = weighted * shrink[..., None] + jnp.einsum(
            "hqk,khd->hqd",
            weights.astype(jnp.bfloat16),
            value_block,
            preferred_element_type=jnp.float32,
        )
        return (new_max, running_total, weighted)

    return lax.cond(key_start < query_start + query_block.shape[0], forward_work, keep_state, state)


def query_grad_tile(
    query_grad,
    query_block,
    cot_block,
    log_total,
    delta,
    query_start,
    key_block,
    value_block,
    key_start,
    scale,
):

    def query_work(query_grad):
        allowed, scores = masked_scores(query_block, key_block, query_start, key_start, scale)
        probs = jnp.where(allowed, jnp.exp(scores - log_total[..., None]), 0.0)
        dprobs = jnp.einsum(
            "qhd,khd->hqk", cot_block, value_block, preferred_element_type=jnp.float32
        )
        dscores = (probs * (dprobs - delta[..., None])).astype(jnp.bfloat16)
        return (
            query_grad
            + jnp.einsum("hqk,khd->hqd", dscores, key_block, preferred_element_type=jnp.float32)
            * scale
        )

    return lax.cond(
        key_start < query_start + query_block.shape[0], query_work, keep_state, query_grad
    )


def key_grad_tile(
    grads,
    query_block,
    cot_block,
    log_total,
    delta,
    query_start,
    key_block,
    value_block,
    key_start,
    scale,
):

    def key_work(grads):
        key_grad, value_grad = grads
        allowed, scores = masked_scores(query_block, key_block, query_start, key_start, scale)
        probs = jnp.where(allowed, jnp.exp(scores - log_total[..., None]), 0.0)
        value_grad = value_grad + jnp.einsum(
            "hqk,qhd->hkd",
            probs.astype(jnp.bfloat16),
            cot_block,
            preferred_element_type=jnp.float32,
        )
        dprobs = jnp.einsum(
            "qhd,khd->hqk", cot_block, value_block, preferred_element_type=jnp.float32
        )
        dscores = (probs * (dprobs - delta[..., None])).astype(jnp.bfloat16)
        key_grad = (
            key_grad
            + jnp.einsum("hqk,qhd->hkd", dscores, query_block, preferred_element_type=jnp.float32)
            * scale
        )
        return (key_grad, value_grad)

    return lax.cond(key_start < query_start + query_block.shape[0], key_work, keep_state, grads)


LANES = 128


def dot(left, right, left_dim, right_dim):
    return lax.dot_general(
        left, right, (((left_dim,), (right_dim,)), ((), ())), preferred_element_type=jnp.float32
    )


def hyena_kernel(
    per_group, mixed, earlier, conv_cot, later, gate_in, gate_out, value_in, cot,
    back_rows, ahead_rows, hyena_out, grad_in, grad_out, grad_value, filter_part,
):
    rows = mixed.shape[0]
    span = 2 * rows
    window = jnp.concatenate([earlier[...], mixed[...]], 0)
    cot_here = conv_cot[...]
    ahead = jnp.concatenate([cot_here, later[...]], 0)
    row_id = lax.broadcasted_iota(jnp.int32, (rows, rows), 0)
    col_id = lax.broadcasted_iota(jnp.int32, (rows, rows), 1)
    flip = (row_id + col_id == rows - 1).astype(jnp.float32).astype(jnp.bfloat16)
    flipped = dot(flip, cot_here, 1, 0)
    lane_group = lax.broadcasted_iota(jnp.int32, (rows, LANES), 1) // per_group
    long_conv = jnp.zeros((rows, LANES), jnp.float32)
    mixed_grad = jnp.zeros((rows, LANES), jnp.float32)

    def toeplitz(row):
        spread = jnp.broadcast_to(row, (rows, span))
        return pltpu.roll(spread, 0, 1, stride=1, stride_axis=0).astype(jnp.bfloat16)

    for number in range(LANES // per_group):
        mine = lane_group == number
        back = toeplitz(back_rows[0, number : number + 1, :])
        long_conv = jnp.where(mine, dot(back, window, 1, 0), long_conv)
        forward = toeplitz(ahead_rows[0, number : number + 1, :])
        mixed_grad = jnp.where(mine, dot(forward, ahead, 1, 0), mixed_grad)
        picked = jnp.where(mine, flipped, 0.0).astype(jnp.bfloat16)
        products = dot(picked, window, 1, 1)
        aligned = pltpu.roll(products, 0, 1, stride=1, stride_axis=0)
        filter_part[0, number : number + 1, :] = jnp.sum(aligned, axis=0, keepdims=True)
    hyena_out[...] = (gate_out[...].astype(jnp.float32) * long_conv).astype(jnp.bfloat16)
    grad_in[...] = (mixed_grad * value_in[...].astype(jnp.float32)).astype(jnp.bfloat16)
    grad_out[...] = (cot[...].astype(jnp.float32) * long_conv).astype(jnp.bfloat16)
    grad_value[...] = (mixed_grad * gate_in[...].astype(jnp.float32)).astype(jnp.bfloat16)


def hyena(mixed, earlier, conv_cot, later, gate_in, gate_out, value_in, cot, mr_filter):
    rows, channels = mixed.shape
    taps, groups = mr_filter.shape
    per_group = channels // groups
    per_step = LANES // per_group
    steps = channels // LANES
    span = 2 * rows
    by_group = mr_filter.T
    blank = jnp.zeros((groups, span - taps), jnp.float32)
    back_rows = jnp.concatenate([blank[:, :1], by_group[:, ::-1], blank[:, 1:]], 1)
    ahead_rows = jnp.concatenate([by_group, blank], 1)
    block = pl.BlockSpec((rows, LANES), lambda step: (0, step))
    per = pl.BlockSpec((1, per_step, span), lambda step: (step, 0, 0))

    def body(*refs):
        hyena_kernel(per_group, *refs)

    wide = jax.ShapeDtypeStruct((rows, channels), jnp.bfloat16)
    *outs, parts = pl.pallas_call(
        body,
        grid=(steps,),
        in_specs=[block] * 8 + [per] * 2,
        out_specs=[block] * 4 + [per],
        out_shape=[wide] * 4 + [jax.ShapeDtypeStruct((steps, per_step, span), jnp.float32)],
        cost_estimate=pl.CostEstimate(
            flops=12 * rows * span * channels * per_step, bytes_accessed=12 * rows * channels * 2,
            transcendentals=0,
        ),
        compiler_params=pltpu.CompilerParams(vmem_limit_bytes=32 * 1024 * 1024),
    )(
        mixed, earlier, conv_cot, later, gate_in, gate_out, value_in, cot,
        back_rows.reshape(steps, per_step, span), ahead_rows.reshape(steps, per_step, span),
    )
    local_grad = parts.reshape(groups, span)[:, span - taps :][:, ::-1].T
    return outs, local_grad


def attention_kernel(block, arrays, results, keys_across, values_across, cots_across, key_sum, value_sum):
    count, _, length, _ = arrays.shape
    total = count * length
    scale = HEAD_DIM ** (-0.5)
    per = block // length

    def take(which, first, last):
        return arrays[first:last, which].reshape((last - first) * length, HEAD_DIM)

    def put(which, first, last, value):
        results[first:last, which] = value.astype(jnp.bfloat16).reshape(
            last - first, length, HEAD_DIM
        )

    keys_across[...] = take(1, 0, count).T
    values_across[...] = take(2, 0, count).T
    cots_across[...] = take(3, 0, count).T
    key_row = lax.broadcasted_iota(jnp.int32, (block, block), 0)
    query_col = lax.broadcasted_iota(jnp.int32, (block, block), 1)
    allowed = key_row <= query_col
    for step in reversed(range(total // block)):
        first, last = step * per, (step + 1) * per
        here = slice(step * block, (step + 1) * block)
        queries, cots = take(0, first, last), take(3, first, last)
        pieces = []
        for part in range(step + 1):
            piece = dot(take(1, part * per, (part + 1) * per), queries, 1, 1) * scale
            pieces.append(jnp.where(allowed, piece, NEG) if part == step else piece)
        row_max = pieces[0].max(axis=0, keepdims=True)
        for piece in pieces[1:]:
            row_max = jnp.maximum(row_max, piece.max(axis=0, keepdims=True))
        probs = [jnp.exp(piece - row_max) for piece in pieces]
        row_total = probs[0].sum(axis=0, keepdims=True)
        for piece in probs[1:]:
            row_total = row_total + piece.sum(axis=0, keepdims=True)
        weighted = None
        for part, piece in enumerate(probs):
            span = slice(part * block, (part + 1) * block)
            term = dot(values_across[:, span], piece.astype(jnp.bfloat16), 1, 0)
            weighted = term if weighted is None else weighted + term
        inverse = 1.0 / row_total
        output = (weighted * inverse).astype(jnp.bfloat16).astype(jnp.float32)
        put(0, first, last, output.T)
        delta = jnp.sum(cots_across[:, here].astype(jnp.float32) * output, axis=0, keepdims=True)
        query_grad = None
        for part, piece in enumerate(probs):
            span = slice(part * block, (part + 1) * block)
            piece = piece * inverse
            value_term = dot(piece.astype(jnp.bfloat16), cots, 1, 0)
            dprobs = dot(take(2, part * per, (part + 1) * per), cots, 1, 1)
            dscores = (piece * (dprobs - delta)).astype(jnp.bfloat16)
            key_term = dot(dscores, queries, 1, 0)
            if step == total // block - 1:
                value_sum[span], key_sum[span] = value_term, key_term
            else:
                value_sum[span] += value_term
                key_sum[span] += key_term
            term = dot(keys_across[:, span], dscores, 1, 0)
            query_grad = term if query_grad is None else query_grad + term
        put(1, first, last, (query_grad * scale).T)
    put(2, 0, count, key_sum[...] * scale)
    put(3, 0, count, value_sum[...])


def pack_kernel(*refs):
    *sources, packed = refs
    for which, source in enumerate(sources):
        for head in range(packed.shape[0]):
            packed[head, which] = source[:, head * HEAD_DIM : (head + 1) * HEAD_DIM]


def unpack_kernel(packed, *targets):
    for which, target in enumerate(targets):
        for head in range(packed.shape[0]):
            target[:, head * HEAD_DIM : (head + 1) * HEAD_DIM] = packed[head, which]


def repacked(kernel, arrays, out_shape, length, heads, packed_in):
    per = max(1, heads // 4)
    flat = pl.BlockSpec((length, per * HEAD_DIM), lambda step: (0, step))
    packed = pl.BlockSpec((per, 4, length, HEAD_DIM), lambda step: (step, 0, 0, 0))
    return pl.pallas_call(
        kernel,
        grid=(heads // per,),
        in_specs=[packed] if packed_in else [flat] * 4,
        out_specs=[flat] * 4 if packed_in else packed,
        out_shape=out_shape,
        cost_estimate=pl.CostEstimate(
            flops=0, bytes_accessed=16 * length * heads * HEAD_DIM, transcendentals=0
        ),
        compiler_params=pltpu.CompilerParams(vmem_limit_bytes=32 * 1024 * 1024),
    )(*arrays)


def heads_sent(queries, keys, values, attn_cot):
    peers = lax.axis_size("ctx")
    length = queries.shape[0]
    shape = jax.ShapeDtypeStruct((peers, 4, length, HEAD_DIM), jnp.bfloat16)
    packed = repacked(
        pack_kernel, (queries, keys, values, attn_cot), shape, length, peers, False
    )
    return lax.all_to_all(packed, "ctx", 0, 0)


def whole_head(arrays):
    peers, _, length, _ = arrays.shape
    total = peers * length
    across = pltpu.VMEM((HEAD_DIM, total), jnp.bfloat16)
    down = pltpu.VMEM((total, HEAD_DIM), jnp.float32)

    def body(*refs):
        attention_kernel(2 * length, *refs)

    return pl.pallas_call(
        body,
        in_specs=[pl.BlockSpec(memory_space=pltpu.VMEM)],
        out_specs=pl.BlockSpec(memory_space=pltpu.VMEM),
        out_shape=jax.ShapeDtypeStruct(arrays.shape, jnp.bfloat16),
        scratch_shapes=[across] * 3 + [down] * 2,
        cost_estimate=pl.CostEstimate(
            flops=7 * total * total * HEAD_DIM, bytes_accessed=16 * total * HEAD_DIM,
            transcendentals=total * total // 2,
        ),
        compiler_params=pltpu.CompilerParams(vmem_limit_bytes=48 * 1024 * 1024),
    )(arrays)


def heads_back(results):
    peers, _, length, _ = results.shape
    results = lax.all_to_all(results, "ctx", 0, 0)
    shape = [jax.ShapeDtypeStruct((length, peers * HEAD_DIM), jnp.bfloat16)] * 4
    return repacked(unpack_kernel, (results,), shape, length, peers, True)


def ring_attention(queries, keys, values, attn_cot):
    position = lax.axis_index("ctx")
    stacked = jnp.stack([queries, keys, values, attn_cot])
    for bit in (0, 1):
        stacked = heads_in(stacked, position, bit)
    bits = lax.axis_size("ctx").bit_length() - 1
    stacked = fold_rows(stacked, bits)
    rows = stacked.shape[1]
    length = rows // 2
    heads_here = stacked.shape[2] // HEAD_DIM
    split = stacked.reshape(4, rows, heads_here, HEAD_DIM)
    query_here = split[0]
    key_here = split[1]
    value_here = split[2]
    cot_here = split[3]
    group_count = lax.axis_size("ctx") // 4
    group = position // 4
    mine = block_starts(group, length, group_count)
    scale = HEAD_DIM ** (-0.5)
    query_blocks = (query_here[:length], query_here[length:])
    cot_blocks = (cot_here[:length], cot_here[length:])

    def forward_visit(states, pair, source):
        theirs = block_starts(source, length, group_count)
        updated = []
        for query_side in (0, 1):
            state = states[query_side]
            for key_side in (0, 1):
                state = forward_tile(
                    state,
                    query_blocks[query_side],
                    mine[query_side],
                    pair[0, key_side * length : (key_side + 1) * length],
                    pair[1, key_side * length : (key_side + 1) * length],
                    theirs[key_side],
                    scale,
                )
            updated.append(state)
        return tuple(updated)

    empty = (
        jnp.full((heads_here, length), NEG, jnp.float32),
        jnp.zeros((heads_here, length), jnp.float32),
        jnp.zeros((heads_here, length, HEAD_DIM), jnp.float32),
    )
    pair = jnp.stack([key_here, value_here])
    saved = jnp.zeros((group_count,) + pair.shape, jnp.bfloat16)

    def forward_step(step, carry):
        states, saved, pair = carry
        states = forward_visit(states, pair, (group - step) % group_count)
        saved = lax.dynamic_update_index_in_dim(saved, pair, step, 0)
        pair = from_behind(pair, "ctx", 4)
        return (states, saved, pair)

    states, saved, pair = lax.fori_loop(
        0, group_count - 1, forward_step, ((empty, empty), saved, pair)
    )
    final_step = group_count - 1
    states = forward_visit(states, pair, (group - final_step) % group_count)
    saved = lax.dynamic_update_index_in_dim(saved, pair, final_step, 0)
    out_blocks = []
    log_totals = []
    deltas = []
    for query_side in (0, 1):
        running_max, running_total, weighted = states[query_side]
        output = (weighted / running_total[..., None]).astype(jnp.bfloat16)
        out_blocks.append(output)
        log_totals.append(running_max + jnp.log(running_total))
        cot_heads = jnp.transpose(cot_blocks[query_side], (1, 0, 2)).astype(jnp.float32)
        deltas.append(jnp.sum(cot_heads * output.astype(jnp.float32), axis=-1))
    zero_grad = jnp.zeros((heads_here, length, HEAD_DIM), jnp.float32)

    def query_step(step, grads):
        pair = lax.dynamic_index_in_dim(saved, step, 0, keepdims=False)
        theirs = block_starts((group - step) % group_count, length, group_count)
        updated = []
        for query_side in (0, 1):
            current = grads[query_side]
            for key_side in (0, 1):
                current = query_grad_tile(
                    current,
                    query_blocks[query_side],
                    cot_blocks[query_side],
                    log_totals[query_side],
                    deltas[query_side],
                    mine[query_side],
                    pair[0, key_side * length : (key_side + 1) * length],
                    pair[1, key_side * length : (key_side + 1) * length],
                    theirs[key_side],
                    scale,
                )
            updated.append(current)
        return tuple(updated)

    query_grads = lax.fori_loop(0, group_count, query_step, (zero_grad, zero_grad))

    def key_visit(grads, packed, log_all, delta_all, source):
        theirs = block_starts(source, length, group_count)
        updated = []
        for key_side in (0, 1):
            current = grads[key_side]
            for query_side in (0, 1):
                current = key_grad_tile(
                    current,
                    packed[0, query_side * length : (query_side + 1) * length],
                    packed[1, query_side * length : (query_side + 1) * length],
                    log_all[query_side],
                    delta_all[query_side],
                    theirs[query_side],
                    key_here[key_side * length : (key_side + 1) * length],
                    value_here[key_side * length : (key_side + 1) * length],
                    mine[key_side],
                    scale,
                )
            updated.append(current)
        return tuple(updated)

    def key_step(step, carry):
        grads, packed, log_all, delta_all = carry
        grads = key_visit(grads, packed, log_all, delta_all, (group - step) % group_count)
        packed = from_behind(packed, "ctx", 4)
        log_all, delta_all = from_behind((log_all, delta_all), "ctx", 4)
        return (grads, packed, log_all, delta_all)

    start_grads = ((zero_grad, zero_grad), (zero_grad, zero_grad))
    packed = jnp.stack([query_here, cot_here])
    carry = (start_grads, packed, jnp.stack(log_totals), jnp.stack(deltas))
    grads, packed, log_all, delta_all = lax.fori_loop(0, group_count - 1, key_step, carry)
    grads = key_visit(grads, packed, log_all, delta_all, (group - final_step) % group_count)

    def joined_rows(first_block, second_block):
        whole = jnp.concatenate([first_block, second_block], 1)
        return jnp.transpose(whole, (1, 0, 2)).reshape(rows, -1).astype(jnp.bfloat16)

    result = jnp.stack(
        [
            joined_rows(out_blocks[0], out_blocks[1]),
            joined_rows(query_grads[0], query_grads[1]),
            joined_rows(grads[0][0], grads[1][0]),
            joined_rows(grads[0][1], grads[1][1]),
        ]
    )
    result = fold_rows(result, bits)
    for bit in (1, 0):
        result = heads_out(result, position, bit)
    return result[0], result[1], result[2], result[3]


def summed_over(value, axis):
    step = 1
    while step < lax.axis_size(axis):
        pairs = [(i, i ^ step) for i in range(lax.axis_size(axis))]
        value = value + lax.ppermute(value, axis, pairs)
        step *= 2
    return value


def partial_rows(tokens, feature_table):
    vocab_part = feature_table.shape[0]
    first_id = lax.axis_index("ch") * vocab_part
    matches = tokens[:, None] == first_id + lax.iota(jnp.int32, vocab_part)[None, :]
    return jnp.einsum(
        "tv,vic->itc",
        matches.astype(jnp.bfloat16),
        feature_table,
        preferred_element_type=jnp.float32,
    ).astype(jnp.bfloat16)


def hyena_layer(gates, hyena_cot, mr_filter):
    gate_in, gate_out, value_in = gates
    mixed = (gate_in.astype(jnp.float32) * value_in.astype(jnp.float32)).astype(jnp.bfloat16)
    conv_cot = (hyena_cot.astype(jnp.float32) * gate_out.astype(jnp.float32)).astype(jnp.bfloat16)
    earlier = passed_along(mixed, "ctx", 1)
    later = passed_along(conv_cot, "ctx", -1)
    outs, local_grad = hyena(
        mixed, earlier, conv_cot, later, gate_in, gate_out, value_in, hyena_cot, mr_filter
    )
    return outs[0], jnp.stack(outs[1:], axis=1), local_grad


def local(tokens, feature_table, mr_filter, hyena_cot, queries, keys, values, attn_cot):
    partial = partial_rows(tokens, feature_table)
    rows = (queries, keys, values, attn_cot)
    if lax.axis_size("ch") != 2 or queries.shape[1] != lax.axis_size("ctx") * HEAD_DIM:
        gates = lax.psum_scatter(partial, "ch", scatter_dimension=2, tiled=True)
        hyena_out, feat_grads, local_grad = hyena_layer(gates, hyena_cot, mr_filter)
        return (hyena_out, feat_grads, summed_over(local_grad, "ctx"), *ring_attention(*rows))
    width = partial.shape[2] // 2
    upper = lax.axis_index("ch") == 1
    low, high = partial[:, :, :width], partial[:, :, width:]
    given = jnp.where(upper, low, high)
    given, rows = lax.optimization_barrier((given, rows))
    received = lax.ppermute(given, "ch", [(0, 1), (1, 0)])
    arrays = heads_sent(*rows)
    gates = jnp.where(upper, high, low) + received
    hyena_out, feat_grads, local_grad = hyena_layer(gates, hyena_cot, mr_filter)
    arrays, local_grad = lax.optimization_barrier((arrays, local_grad))
    filter_grad = summed_over(local_grad, "ctx")
    results = whole_head(arrays)
    results, filter_grad = lax.optimization_barrier((results, filter_grad))
    return (hyena_out, feat_grads, filter_grad, *heads_back(results))


def solution(mesh):
    return jax.shard_map(
        local,
        mesh=mesh,
        in_specs=(
            P("ctx"),
            P("ch", None, None),
            P(None, "ch"),
            P("ctx", "ch"),
            P("ctx", "ch"),
            P("ctx", "ch"),
            P("ctx", "ch"),
            P("ctx", "ch"),
        ),
        out_specs=(
            P("ctx", "ch"),
            P("ctx", None, "ch"),
            P(None, "ch"),
            P("ctx", "ch"),
            P("ctx", "ch"),
            P("ctx", "ch"),
            P("ctx", "ch"),
        ),
        check_vma=False,
    )
```

```python
import jax
import jax.numpy as jnp
from jax import lax
from jax.experimental import pallas as pl
from jax.experimental.pallas import tpu as pltpu
from jax.sharding import PartitionSpec as P

HEAD_DIM = 128


NEG = -1e30


def from_partner(shard, axis, apart):
    return lax.ppermute(shard, axis, [(i, i ^ 1 << apart) for i in range(lax.axis_size(axis))])


def passed_along(value, axis, steps):
    count = lax.axis_size(axis)
    leading, last = (max(0, -steps), min(count, count - steps))
    return lax.ppermute(value, axis, [(source, source + steps) for source in range(leading, last)])


def from_behind(shard, axis, by):
    peers = lax.axis_size(axis)
    return lax.ppermute(shard, axis, [(i, (i + by) % peers) for i in range(peers)])


def heads_in(stacked, position, bit):
    width = stacked.shape[2] // 2
    upper = position // (1 << bit) % 2 == 1
    lower_heads = stacked[:, :, :width]
    upper_heads = stacked[:, :, width:]
    kept = jnp.where(upper, upper_heads, lower_heads)
    given = jnp.where(upper, lower_heads, upper_heads)
    received = from_partner(given, "ctx", bit)
    return jnp.concatenate([jnp.where(upper, received, kept), jnp.where(upper, kept, received)], 1)


def heads_out(stacked, position, bit):
    length = stacked.shape[1] // 2
    upper = position // (1 << bit) % 2 == 1
    lower_rows = stacked[:, :length]
    upper_rows = stacked[:, length:]
    kept = jnp.where(upper, upper_rows, lower_rows)
    given = jnp.where(upper, lower_rows, upper_rows)
    received = from_partner(given, "ctx", bit)
    return jnp.concatenate([jnp.where(upper, received, kept), jnp.where(upper, kept, received)], 2)


def fold_rows(stacked, bits):
    length = stacked.shape[1] // 2
    moving = stacked[:, length:]
    for bit in range(2, bits):
        moving = from_partner(moving, "ctx", bit)
    return jnp.concatenate([stacked[:, :length], moving], 1)


def block_starts(group, length, group_count):
    return (2 * group * length, (2 * group_count - 1 - 2 * group) * length)


def masked_scores(query_block, key_block, query_start, key_start, scale):
    query_pos = query_start + lax.iota(jnp.int32, query_block.shape[0])
    key_pos = key_start + lax.iota(jnp.int32, key_block.shape[0])
    allowed = (key_pos[None, :] <= query_pos[:, None])[None]
    scores = (
        jnp.einsum("qhd,khd->hqk", query_block, key_block, preferred_element_type=jnp.float32)
        * scale
    )
    return (allowed, jnp.where(allowed, scores, NEG))


def keep_state(state):
    return state


def forward_tile(state, query_block, query_start, key_block, value_block, key_start, scale):

    def forward_work(state):
        running_max, running_total, weighted = state
        allowed, scores = masked_scores(query_block, key_block, query_start, key_start, scale)
        new_max = jnp.maximum(running_max, scores.max(axis=-1))
        weights = jnp.where(allowed, jnp.exp(scores - new_max[..., None]), 0.0)
        shrink = jnp.exp(running_max - new_max)
        running_total = running_total * shrink + weights.sum(axis=-1)
        weighted = weighted * shrink[..., None] + jnp.einsum(
            "hqk,khd->hqd",
            weights.astype(jnp.bfloat16),
            value_block,
            preferred_element_type=jnp.float32,
        )
        return (new_max, running_total, weighted)

    return lax.cond(key_start < query_start + query_block.shape[0], forward_work, keep_state, state)


def query_grad_tile(
    query_grad,
    query_block,
    cot_block,
    log_total,
    delta,
    query_start,
    key_block,
    value_block,
    key_start,
    scale,
):

    def query_work(query_grad):
        allowed, scores = masked_scores(query_block, key_block, query_start, key_start, scale)
        probs = jnp.where(allowed, jnp.exp(scores - log_total[..., None]), 0.0)
        dprobs = jnp.einsum(
            "qhd,khd->hqk", cot_block, value_block, preferred_element_type=jnp.float32
        )
        dscores = (probs * (dprobs - delta[..., None])).astype(jnp.bfloat16)
        return (
            query_grad
            + jnp.einsum("hqk,khd->hqd", dscores, key_block, preferred_element_type=jnp.float32)
            * scale
        )

    return lax.cond(
        key_start < query_start + query_block.shape[0], query_work, keep_state, query_grad
    )


def key_grad_tile(
    grads,
    query_block,
    cot_block,
    log_total,
    delta,
    query_start,
    key_block,
    value_block,
    key_start,
    scale,
):

    def key_work(grads):
        key_grad, value_grad = grads
        allowed, scores = masked_scores(query_block, key_block, query_start, key_start, scale)
        probs = jnp.where(allowed, jnp.exp(scores - log_total[..., None]), 0.0)
        value_grad = value_grad + jnp.einsum(
            "hqk,qhd->hkd",
            probs.astype(jnp.bfloat16),
            cot_block,
            preferred_element_type=jnp.float32,
        )
        dprobs = jnp.einsum(
            "qhd,khd->hqk", cot_block, value_block, preferred_element_type=jnp.float32
        )
        dscores = (probs * (dprobs - delta[..., None])).astype(jnp.bfloat16)
        key_grad = (
            key_grad
            + jnp.einsum("hqk,qhd->hkd", dscores, query_block, preferred_element_type=jnp.float32)
            * scale
        )
        return (key_grad, value_grad)

    return lax.cond(key_start < query_start + query_block.shape[0], key_work, keep_state, grads)


LANES = 128


def dot(left, right, left_dim, right_dim):
    return lax.dot_general(
        left, right, (((left_dim,), (right_dim,)), ((), ())), preferred_element_type=jnp.float32
    )


def hyena_kernel(
    per_group, mixed, earlier, conv_cot, later, gate_in, gate_out, value_in, cot,
    back_rows, ahead_rows, hyena_out, grad_in, grad_out, grad_value, filter_part,
):
    rows = mixed.shape[0]
    span = 2 * rows
    window = jnp.concatenate([earlier[...], mixed[...]], 0)
    cot_here = conv_cot[...]
    ahead = jnp.concatenate([cot_here, later[...]], 0)
    row_id = lax.broadcasted_iota(jnp.int32, (rows, rows), 0)
    col_id = lax.broadcasted_iota(jnp.int32, (rows, rows), 1)
    flip = (row_id + col_id == rows - 1).astype(jnp.float32).astype(jnp.bfloat16)
    flipped = dot(flip, cot_here, 1, 0)
    lane_group = lax.broadcasted_iota(jnp.int32, (rows, LANES), 1) // per_group
    long_conv = jnp.zeros((rows, LANES), jnp.float32)
    mixed_grad = jnp.zeros((rows, LANES), jnp.float32)

    def toeplitz(row):
        spread = jnp.broadcast_to(row, (rows, span))
        return pltpu.roll(spread, 0, 1, stride=1, stride_axis=0).astype(jnp.bfloat16)

    for number in range(LANES // per_group):
        mine = lane_group == number
        back = toeplitz(back_rows[0, number : number + 1, :])
        long_conv = jnp.where(mine, dot(back, window, 1, 0), long_conv)
        forward = toeplitz(ahead_rows[0, number : number + 1, :])
        mixed_grad = jnp.where(mine, dot(forward, ahead, 1, 0), mixed_grad)
        picked = jnp.where(mine, flipped, 0.0).astype(jnp.bfloat16)
        products = dot(picked, window, 1, 1)
        aligned = pltpu.roll(products, 0, 1, stride=1, stride_axis=0)
        filter_part[0, number : number + 1, :] = jnp.sum(aligned, axis=0, keepdims=True)
    hyena_out[...] = (gate_out[...].astype(jnp.float32) * long_conv).astype(jnp.bfloat16)
    grad_in[...] = (mixed_grad * value_in[...].astype(jnp.float32)).astype(jnp.bfloat16)
    grad_out[...] = (cot[...].astype(jnp.float32) * long_conv).astype(jnp.bfloat16)
    grad_value[...] = (mixed_grad * gate_in[...].astype(jnp.float32)).astype(jnp.bfloat16)


def hyena(mixed, earlier, conv_cot, later, gate_in, gate_out, value_in, cot, mr_filter):
    rows, channels = mixed.shape
    taps, groups = mr_filter.shape
    per_group = channels // groups
    per_step = LANES // per_group
    steps = channels // LANES
    span = 2 * rows
    by_group = mr_filter.T
    blank = jnp.zeros((groups, span - taps), jnp.float32)
    back_rows = jnp.concatenate([blank[:, :1], by_group[:, ::-1], blank[:, 1:]], 1)
    ahead_rows = jnp.concatenate([by_group, blank], 1)
    block = pl.BlockSpec((rows, LANES), lambda step: (0, step))
    per = pl.BlockSpec((1, per_step, span), lambda step: (step, 0, 0))

    def body(*refs):
        hyena_kernel(per_group, *refs)

    wide = jax.ShapeDtypeStruct((rows, channels), jnp.bfloat16)
    *outs, parts = pl.pallas_call(
        body,
        grid=(steps,),
        in_specs=[block] * 8 + [per] * 2,
        out_specs=[block] * 4 + [per],
        out_shape=[wide] * 4 + [jax.ShapeDtypeStruct((steps, per_step, span), jnp.float32)],
        cost_estimate=pl.CostEstimate(
            flops=12 * rows * span * channels * per_step, bytes_accessed=12 * rows * channels * 2,
            transcendentals=0,
        ),
        compiler_params=pltpu.CompilerParams(vmem_limit_bytes=32 * 1024 * 1024),
    )(
        mixed, earlier, conv_cot, later, gate_in, gate_out, value_in, cot,
        back_rows.reshape(steps, per_step, span), ahead_rows.reshape(steps, per_step, span),
    )
    local_grad = parts.reshape(groups, span)[:, span - taps :][:, ::-1].T
    return outs, local_grad


def attention_kernel(block, arrays, results, keys_across, values_across, cots_across, key_sum, value_sum):
    count, _, length, _ = arrays.shape
    total = count * length
    scale = HEAD_DIM ** (-0.5)
    per = block // length

    def take(which, first, last):
        return arrays[first:last, which].reshape((last - first) * length, HEAD_DIM)

    def put(which, first, last, value):
        results[first:last, which] = value.astype(jnp.bfloat16).reshape(
            last - first, length, HEAD_DIM
        )

    keys_across[...] = take(1, 0, count).T
    values_across[...] = take(2, 0, count).T
    cots_across[...] = take(3, 0, count).T
    key_row = lax.broadcasted_iota(jnp.int32, (block, block), 0)
    query_col = lax.broadcasted_iota(jnp.int32, (block, block), 1)
    allowed = key_row <= query_col
    for step in reversed(range(total // block)):
        first, last = step * per, (step + 1) * per
        here = slice(step * block, (step + 1) * block)
        queries, cots = take(0, first, last), take(3, first, last)
        pieces = []
        for part in range(step + 1):
            piece = dot(take(1, part * per, (part + 1) * per), queries, 1, 1) * scale
            pieces.append(jnp.where(allowed, piece, NEG) if part == step else piece)
        row_max = pieces[0].max(axis=0, keepdims=True)
        for piece in pieces[1:]:
            row_max = jnp.maximum(row_max, piece.max(axis=0, keepdims=True))
        probs = [jnp.exp(piece - row_max) for piece in pieces]
        row_total = probs[0].sum(axis=0, keepdims=True)
        for piece in probs[1:]:
            row_total = row_total + piece.sum(axis=0, keepdims=True)
        weighted = None
        for part, piece in enumerate(probs):
            span = slice(part * block, (part + 1) * block)
            term = dot(values_across[:, span], piece.astype(jnp.bfloat16), 1, 0)
            weighted = term if weighted is None else weighted + term
        inverse = 1.0 / row_total
        output = (weighted * inverse).astype(jnp.bfloat16).astype(jnp.float32)
        put(0, first, last, output.T)
        delta = jnp.sum(cots_across[:, here].astype(jnp.float32) * output, axis=0, keepdims=True)
        query_grad = None
        for part, piece in enumerate(probs):
            span = slice(part * block, (part + 1) * block)
            piece = piece * inverse
            value_term = dot(piece.astype(jnp.bfloat16), cots, 1, 0)
            dprobs = dot(take(2, part * per, (part + 1) * per), cots, 1, 1)
            dscores = (piece * (dprobs - delta)).astype(jnp.bfloat16)
            key_term = dot(dscores, queries, 1, 0)
            if step == total // block - 1:
                value_sum[span], key_sum[span] = value_term, key_term
            else:
                value_sum[span] += value_term
                key_sum[span] += key_term
            term = dot(keys_across[:, span], dscores, 1, 0)
            query_grad = term if query_grad is None else query_grad + term
        put(1, first, last, (query_grad * scale).T)
    put(2, 0, count, key_sum[...] * scale)
    put(3, 0, count, value_sum[...])


def pack_kernel(*refs):
    *sources, packed = refs
    for which, source in enumerate(sources):
        for head in range(packed.shape[0]):
            packed[head, which] = source[:, head * HEAD_DIM : (head + 1) * HEAD_DIM]


def unpack_kernel(packed, *targets):
    for which, target in enumerate(targets):
        for head in range(packed.shape[0]):
            target[:, head * HEAD_DIM : (head + 1) * HEAD_DIM] = packed[head, which]


def repacked(kernel, arrays, out_shape, length, heads, packed_in):
    per = max(1, heads // 4)
    flat = pl.BlockSpec((length, per * HEAD_DIM), lambda step: (0, step))
    packed = pl.BlockSpec((per, 4, length, HEAD_DIM), lambda step: (step, 0, 0, 0))
    return pl.pallas_call(
        kernel,
        grid=(heads // per,),
        in_specs=[packed] if packed_in else [flat] * 4,
        out_specs=[flat] * 4 if packed_in else packed,
        out_shape=out_shape,
        cost_estimate=pl.CostEstimate(
            flops=0, bytes_accessed=16 * length * heads * HEAD_DIM, transcendentals=0
        ),
        compiler_params=pltpu.CompilerParams(vmem_limit_bytes=32 * 1024 * 1024),
    )(*arrays)


def heads_sent(queries, keys, values, attn_cot):
    peers = lax.axis_size("ctx")
    length = queries.shape[0]
    shape = jax.ShapeDtypeStruct((peers, 4, length, HEAD_DIM), jnp.bfloat16)
    packed = repacked(
        pack_kernel, (queries, keys, values, attn_cot), shape, length, peers, False
    )
    return lax.all_to_all(packed, "ctx", 0, 0)


def whole_head(arrays):
    peers, _, length, _ = arrays.shape
    total = peers * length
    across = pltpu.VMEM((HEAD_DIM, total), jnp.bfloat16)
    down = pltpu.VMEM((total, HEAD_DIM), jnp.float32)

    def body(*refs):
        attention_kernel(2 * length, *refs)

    return pl.pallas_call(
        body,
        in_specs=[pl.BlockSpec(memory_space=pltpu.VMEM)],
        out_specs=pl.BlockSpec(memory_space=pltpu.VMEM),
        out_shape=jax.ShapeDtypeStruct(arrays.shape, jnp.bfloat16),
        scratch_shapes=[across] * 3 + [down] * 2,
        cost_estimate=pl.CostEstimate(
            flops=7 * total * total * HEAD_DIM, bytes_accessed=16 * total * HEAD_DIM,
            transcendentals=total * total // 2,
        ),
        compiler_params=pltpu.CompilerParams(vmem_limit_bytes=48 * 1024 * 1024),
    )(arrays)


def heads_back(results):
    peers, _, length, _ = results.shape
    shape = [jax.ShapeDtypeStruct((length, peers * HEAD_DIM), jnp.bfloat16)] * 4
    return repacked(unpack_kernel, (results,), shape, length, peers, True)


def ring_attention(queries, keys, values, attn_cot):
    position = lax.axis_index("ctx")
    stacked = jnp.stack([queries, keys, values, attn_cot])
    for bit in (0, 1):
        stacked = heads_in(stacked, position, bit)
    bits = lax.axis_size("ctx").bit_length() - 1
    stacked = fold_rows(stacked, bits)
    rows = stacked.shape[1]
    length = rows // 2
    heads_here = stacked.shape[2] // HEAD_DIM
    split = stacked.reshape(4, rows, heads_here, HEAD_DIM)
    query_here = split[0]
    key_here = split[1]
    value_here = split[2]
    cot_here = split[3]
    group_count = lax.axis_size("ctx") // 4
    group = position // 4
    mine = block_starts(group, length, group_count)
    scale = HEAD_DIM ** (-0.5)
    query_blocks = (query_here[:length], query_here[length:])
    cot_blocks = (cot_here[:length], cot_here[length:])

    def forward_visit(states, pair, source):
        theirs = block_starts(source, length, group_count)
        updated = []
        for query_side in (0, 1):
            state = states[query_side]
            for key_side in (0, 1):
                state = forward_tile(
                    state,
                    query_blocks[query_side],
                    mine[query_side],
                    pair[0, key_side * length : (key_side + 1) * length],
                    pair[1, key_side * length : (key_side + 1) * length],
                    theirs[key_side],
                    scale,
                )
            updated.append(state)
        return tuple(updated)

    empty = (
        jnp.full((heads_here, length), NEG, jnp.float32),
        jnp.zeros((heads_here, length), jnp.float32),
        jnp.zeros((heads_here, length, HEAD_DIM), jnp.float32),
    )
    pair = jnp.stack([key_here, value_here])
    saved = jnp.zeros((group_count,) + pair.shape, jnp.bfloat16)

    def forward_step(step, carry):
        states, saved, pair = carry
        states = forward_visit(states, pair, (group - step) % group_count)
        saved = lax.dynamic_update_index_in_dim(saved, pair, step, 0)
        pair = from_behind(pair, "ctx", 4)
        return (states, saved, pair)

    states, saved, pair = lax.fori_loop(
        0, group_count - 1, forward_step, ((empty, empty), saved, pair)
    )
    final_step = group_count - 1
    states = forward_visit(states, pair, (group - final_step) % group_count)
    saved = lax.dynamic_update_index_in_dim(saved, pair, final_step, 0)
    out_blocks = []
    log_totals = []
    deltas = []
    for query_side in (0, 1):
        running_max, running_total, weighted = states[query_side]
        output = (weighted / running_total[..., None]).astype(jnp.bfloat16)
        out_blocks.append(output)
        log_totals.append(running_max + jnp.log(running_total))
        cot_heads = jnp.transpose(cot_blocks[query_side], (1, 0, 2)).astype(jnp.float32)
        deltas.append(jnp.sum(cot_heads * output.astype(jnp.float32), axis=-1))
    zero_grad = jnp.zeros((heads_here, length, HEAD_DIM), jnp.float32)

    def query_step(step, grads):
        pair = lax.dynamic_index_in_dim(saved, step, 0, keepdims=False)
        theirs = block_starts((group - step) % group_count, length, group_count)
        updated = []
        for query_side in (0, 1):
            current = grads[query_side]
            for key_side in (0, 1):
                current = query_grad_tile(
                    current,
                    query_blocks[query_side],
                    cot_blocks[query_side],
                    log_totals[query_side],
                    deltas[query_side],
                    mine[query_side],
                    pair[0, key_side * length : (key_side + 1) * length],
                    pair[1, key_side * length : (key_side + 1) * length],
                    theirs[key_side],
                    scale,
                )
            updated.append(current)
        return tuple(updated)

    query_grads = lax.fori_loop(0, group_count, query_step, (zero_grad, zero_grad))

    def key_visit(grads, packed, log_all, delta_all, source):
        theirs = block_starts(source, length, group_count)
        updated = []
        for key_side in (0, 1):
            current = grads[key_side]
            for query_side in (0, 1):
                current = key_grad_tile(
                    current,
                    packed[0, query_side * length : (query_side + 1) * length],
                    packed[1, query_side * length : (query_side + 1) * length],
                    log_all[query_side],
                    delta_all[query_side],
                    theirs[query_side],
                    key_here[key_side * length : (key_side + 1) * length],
                    value_here[key_side * length : (key_side + 1) * length],
                    mine[key_side],
                    scale,
                )
            updated.append(current)
        return tuple(updated)

    def key_step(step, carry):
        grads, packed, log_all, delta_all = carry
        grads = key_visit(grads, packed, log_all, delta_all, (group - step) % group_count)
        packed = from_behind(packed, "ctx", 4)
        log_all, delta_all = from_behind((log_all, delta_all), "ctx", 4)
        return (grads, packed, log_all, delta_all)

    start_grads = ((zero_grad, zero_grad), (zero_grad, zero_grad))
    packed = jnp.stack([query_here, cot_here])
    carry = (start_grads, packed, jnp.stack(log_totals), jnp.stack(deltas))
    grads, packed, log_all, delta_all = lax.fori_loop(0, group_count - 1, key_step, carry)
    grads = key_visit(grads, packed, log_all, delta_all, (group - final_step) % group_count)

    def joined_rows(first_block, second_block):
        whole = jnp.concatenate([first_block, second_block], 1)
        return jnp.transpose(whole, (1, 0, 2)).reshape(rows, -1).astype(jnp.bfloat16)

    result = jnp.stack(
        [
            joined_rows(out_blocks[0], out_blocks[1]),
            joined_rows(query_grads[0], query_grads[1]),
            joined_rows(grads[0][0], grads[1][0]),
            joined_rows(grads[0][1], grads[1][1]),
        ]
    )
    result = fold_rows(result, bits)
    for bit in (1, 0):
        result = heads_out(result, position, bit)
    return result[0], result[1], result[2], result[3]


def summed_over(value, axis):
    step = 1
    while step < lax.axis_size(axis):
        pairs = [(i, i ^ step) for i in range(lax.axis_size(axis))]
        value = value + lax.ppermute(value, axis, pairs)
        step *= 2
    return value


def partial_rows(tokens, feature_table):
    vocab_part = feature_table.shape[0]
    first_id = lax.axis_index("ch") * vocab_part
    matches = tokens[:, None] == first_id + lax.iota(jnp.int32, vocab_part)[None, :]
    return jnp.einsum(
        "tv,vic->itc",
        matches.astype(jnp.bfloat16),
        feature_table,
        preferred_element_type=jnp.float32,
    ).astype(jnp.bfloat16)


def hyena_layer(gates, hyena_cot, mr_filter):
    gate_in, gate_out, value_in = gates
    mixed = (gate_in.astype(jnp.float32) * value_in.astype(jnp.float32)).astype(jnp.bfloat16)
    conv_cot = (hyena_cot.astype(jnp.float32) * gate_out.astype(jnp.float32)).astype(jnp.bfloat16)
    earlier = passed_along(mixed, "ctx", 1)
    later = passed_along(conv_cot, "ctx", -1)
    outs, local_grad = hyena(
        mixed, earlier, conv_cot, later, gate_in, gate_out, value_in, hyena_cot, mr_filter
    )
    return outs[0], jnp.stack(outs[1:], axis=1), local_grad


def local(tokens, feature_table, mr_filter, hyena_cot, queries, keys, values, attn_cot):
    partial = partial_rows(tokens, feature_table)
    rows = (queries, keys, values, attn_cot)
    if lax.axis_size("ch") != 2 or queries.shape[1] != lax.axis_size("ctx") * HEAD_DIM:
        gates = lax.psum_scatter(partial, "ch", scatter_dimension=2, tiled=True)
        hyena_out, feat_grads, local_grad = hyena_layer(gates, hyena_cot, mr_filter)
        return (hyena_out, feat_grads, summed_over(local_grad, "ctx"), *ring_attention(*rows))
    width = partial.shape[2] // 2
    upper = lax.axis_index("ch") == 1
    low, high = partial[:, :, :width], partial[:, :, width:]
    given = jnp.where(upper, low, high)
    given, rows = lax.optimization_barrier((given, rows))
    received = lax.ppermute(given, "ch", [(0, 1), (1, 0)])
    results = whole_head(heads_sent(*rows))
    returned = lax.all_to_all(results, "ctx", 0, 0)
    received, _ = lax.optimization_barrier((received, results))
    gates = jnp.where(upper, high, low) + received
    hyena_out, feat_grads, local_grad = hyena_layer(gates, hyena_cot, mr_filter)
    local_grad, _ = lax.optimization_barrier((local_grad, returned))
    filter_grad = summed_over(local_grad, "ctx")
    return (hyena_out, feat_grads, filter_grad, *heads_back(returned))


def solution(mesh):
    return jax.shard_map(
        local,
        mesh=mesh,
        in_specs=(
            P("ctx"),
            P("ch", None, None),
            P(None, "ch"),
            P("ctx", "ch"),
            P("ctx", "ch"),
            P("ctx", "ch"),
            P("ctx", "ch"),
            P("ctx", "ch"),
        ),
        out_specs=(
            P("ctx", "ch"),
            P("ctx", None, "ch"),
            P(None, "ch"),
            P("ctx", "ch"),
            P("ctx", "ch"),
            P("ctx", "ch"),
            P("ctx", "ch"),
        ),
        check_vma=False,
    )
```
